32 devices in a mesh: groups: 2 (over y), tensor: 8 (over z, x), dp: 2 (over core).
Axes of the slice: x: 2, y: 2, z: 4, core: 2. Of those that a mesh axis runs over, the one named last changes fastest.
Arguments:
- tokens: bfloat16 [512, 8192], P(('groups', 'dp'), 'tensor'), parts along dimension 0, may hold values from -6 to 6
- gate_weight: bfloat16 [8192, 16384], P('dp', 'tensor'), may hold values from -0.09375 to 0.09375
- up_weight: bfloat16 [8192, 16384], P('dp', 'tensor'), may hold values from -0.09375 to 0.09375
- gate_mask: int32 [128, 256], P('dp', 'tensor'), may hold values from 0 to 1, as said below
- up_mask: int32 [128, 256], P('dp', 'tensor'), may hold values from 0 to 1, as said below
- cotangent: bfloat16 [512, 16384], P(('groups', 'dp'), 'tensor'), parts along dimension 0, may hold values from -6 to 6
Outputs:
- hidden: bfloat16 [512, 16384], P(('groups', 'dp'), 'tensor'), parts along dimension 0
- grad_input: bfloat16 [512, 8192], P(('groups', 'dp'), 'tensor'), parts along dimension 0
- grad_gate: bfloat16 [8192, 32768], P('dp', ('groups', 'tensor')), parts along dimension 1
- grad_up: bfloat16 [8192, 32768], P('dp', ('groups', 'tensor')), parts along dimension 1
The draws below stay inside these ranges and needn't reach their ends.
There are 2 independent parts, one for each index of `groups`. The reference program is written for one: setup_inputs(seed, part) draws one part's arguments, and reference() takes and returns one part's arrays. A program takes and returns all parts, laid end to end along the dimension named above; an argument that names none is the same for every part. Nothing has to cross between parts.
Inputs may be any that keep to these rules, and one draw needn't show every extreme that they name: `gate_mask`: each entry says whether a block of 64 x 64 weights is kept (1) or zero (0); the share kept differs from block column to block column. `up_mask`: as gate_mask, drawn independently.
All inputs are finite; a program needn't handle non-finite values.
Results may differ from the reference program's by a relative error of at most 0.005.
Values may be sent and summed in bfloat16 or wider, within the bound.
A program may use at most 320 MiB of HBM per device.

```python
import jax
import jax.numpy as jnp

D = 8192
FF = 16384
BLOCK = 64
TOKENS = 256


def block_table(key):
    first, second = jax.random.split(key)
    density = jax.random.randint(first, (1, FF // BLOCK), 200, 800)
    ticket = jax.random.randint(second, (D // BLOCK, FF // BLOCK), 0, 1000)
    return (ticket < density).astype(jnp.int32)


def draw_gate_mask(key, part):
    key = jax.random.fold_in(key, 11)
    return block_table(key)


def draw_up_mask(key, part):
    key = jax.random.fold_in(key, 23)
    return block_table(key)


def raised(values, stream_key, source, target, shards_of, factor):
    def block_of(dim):
        return (jnp.arange(values.shape[dim]) // (values.shape[dim] // shards_of)).reshape((-1,) + (1,) * (values.ndim - 1 - dim))

    near = jax.random.permutation(stream_key, shards_of)[block_of(target)]
    far = (block_of(target) + shards_of // 2) % shards_of
    return jnp.where((block_of(source) == near) | (block_of(source) == far), factor * values, values)


def block_levels(own_key, shape, cuts, least, top_value):
    loudness, own = 1.0, jax.random.fold_in(own_key, 6)
    for axis_at, blocks in cuts:
        heights = jnp.exp(jax.random.uniform(jax.random.fold_in(own, axis_at), (blocks,), jnp.float32, least / len(cuts), top_value / len(cuts)))
        loudness = loudness * jnp.repeat(heights, shape[axis_at] // blocks).reshape([-1 if axis == axis_at else 1 for axis in range(len(shape))])
    return loudness


def scatter_about(own_key, dims, spread, most, pieces=(), kind=jnp.bfloat16):
    loudness = block_levels(own_key, dims, pieces, -0.22, 0.18) if pieces else 1.0
    values = jax.random.normal(own_key, dims, jnp.float32) * spread * loudness
    return jnp.minimum(jnp.maximum(values, -most), most).astype(kind)


def gaussian_with(rng, dims, spread, most, cuts, heavy, held_as=jnp.bfloat16):
    array = spread * jax.random.normal(rng, dims, jnp.float32)
    if cuts:
        array = array * block_levels(rng, dims, cuts, -0.22, 0.18)
    return jnp.clip(raised(array, jax.random.fold_in(rng, 3), *heavy), -most, most).astype(held_as)


def setup_inputs(seed: int = 0, part: int = 0) -> dict:
    splits = jax.random.split(jax.random.key(seed), 7)
    part_keys = jax.random.split(jax.random.fold_in(splits[6], part), 7)
    return {
        "tokens": scatter_about(part_keys[0], (TOKENS, D), 1.0, 6.0, ((0, 2), (1, 8))),
        "gate_weight": gaussian_with(splits[1], (D, FF), D ** -0.5, 0.09375, ((0, 2), (1, 8)), (1, 0, 8, 2.0)),
        "up_weight": gaussian_with(splits[2], (D, FF), D ** -0.5, 0.09375, ((0, 2), (1, 8)), (1, 0, 8, 2.0)),
        "gate_mask": draw_gate_mask(jax.random.fold_in(splits[6], 71), part),
        "up_mask": draw_up_mask(jax.random.fold_in(splits[6], 71), part),
        "cotangent": scatter_about(part_keys[5], (TOKENS, FF), 1.0, 6.0, ((0, 2), (1, 8))),
    }


def expand_blocks(mask):
    wide = jnp.repeat(jnp.repeat(mask, BLOCK, axis=0), BLOCK, axis=1)
    return wide.astype(jnp.bfloat16)


def reference(tokens, gate_weight, up_weight, gate_mask, up_mask, cotangent):
    gate_wide = expand_blocks(gate_mask)
    up_wide = expand_blocks(up_mask)
    gate_kept = gate_weight * gate_wide
    up_kept = up_weight * up_wide
    gate = jnp.dot(tokens, gate_kept, preferred_element_type=jnp.float32)
    up = jnp.dot(tokens, up_kept, preferred_element_type=jnp.float32)
    sig = jax.nn.sigmoid(gate)
    act = gate * sig
    hidden = (act * up).astype(jnp.bfloat16)
    grad_out = cotangent.astype(jnp.float32)
    d_gate = (grad_out * up * sig * (1.0 + gate * (1.0 - sig))).astype(jnp.bfloat16)
    d_up = (grad_out * act).astype(jnp.bfloat16)
    grad_input = jnp.dot(d_gate, gate_kept.T, preferred_element_type=jnp.float32)
    grad_input = grad_input + jnp.dot(d_up, up_kept.T, preferred_element_type=jnp.float32)
    grad_gate = jnp.dot(tokens.T, d_gate, preferred_element_type=jnp.float32) * gate_wide.astype(jnp.float32)
    grad_up = jnp.dot(tokens.T, d_up, preferred_element_type=jnp.float32) * up_wide.astype(jnp.float32)
    return hidden, grad_input.astype(jnp.bfloat16), grad_gate.astype(jnp.bfloat16), grad_up.astype(jnp.bfloat16)
```

```python
import jax
import jax.numpy as jnp
from jax import lax
from jax.experimental import pallas as pl
from jax.experimental.pallas import tpu as pltpu
from jax.sharding import PartitionSpec as P

BLOCK = 64


def expand_blocks(mask):
    rows, cols = mask.shape
    width = cols * BLOCK
    col_ids = lax.broadcasted_iota(jnp.int32, (cols, width), 1) // BLOCK
    own_ids = lax.broadcasted_iota(jnp.int32, (cols, width), 0)
    spread = (col_ids == own_ids).astype(jnp.bfloat16)
    wide_cols = jnp.dot(
        mask.astype(jnp.bfloat16), spread, preferred_element_type=jnp.float32
    ).astype(jnp.bfloat16)
    wide = jnp.broadcast_to(wide_cols[:, None, :], (rows, BLOCK, width))
    return wide.reshape(rows * BLOCK, width)


def shards(tokens, gate_weight, up_weight, gate_mask, up_mask, cotangent):
    gate_wide = expand_blocks(gate_mask)
    up_wide = expand_blocks(up_mask)
    gate_kept = gate_weight * gate_wide
    up_kept = up_weight * up_wide
    own_rows = lax.all_gather(tokens, "tensor", axis=1, tiled=True)
    half_block = lax.all_to_all(own_rows, "dp", split_axis=1, concat_axis=0, tiled=True)
    gate_full, up_full = (
        lax.all_gather(gate_kept, "dp", axis=0, tiled=True),
        lax.all_gather(up_kept, "dp", axis=0, tiled=True),
    )
    gate = jnp.dot(own_rows, gate_full, preferred_element_type=jnp.float32)
    up = jnp.dot(own_rows, up_full, preferred_element_type=jnp.float32)
    sig = jax.nn.sigmoid(gate)
    act = gate * sig
    hidden = (act * up).astype(jnp.bfloat16)
    grad_out = cotangent.astype(jnp.float32)
    d_gate = (grad_out * up * sig * (1.0 + gate * (1.0 - sig))).astype(jnp.bfloat16)
    d_up = (grad_out * act).astype(jnp.bfloat16)
    gate_all, up_all = (
        lax.all_gather(d_gate, "dp", axis=0, tiled=True),
        lax.all_gather(d_up, "dp", axis=0, tiled=True),
    )
    total = jnp.einsum("dh,th->dt", gate_full, d_gate, preferred_element_type=jnp.float32)
    input_terms = lax.psum_scatter(
        total + jnp.einsum("dh,th->dt", up_full, d_up, preferred_element_type=jnp.float32),
        "tensor",
        scatter_dimension=0,
        tiled=True,
    )
    grad_input = input_terms.T.astype(jnp.bfloat16)
    grad_gate = jnp.einsum("td,th->dh", half_block, gate_all, preferred_element_type=jnp.float32)
    grad_up = jnp.einsum("td,th->dh", half_block, up_all, preferred_element_type=jnp.float32)
    grad_gate = (grad_gate * gate_wide.astype(jnp.float32)).astype(jnp.bfloat16)
    grad_up = (grad_up * up_wide.astype(jnp.float32)).astype(jnp.bfloat16)
    return (hidden, grad_input, grad_gate, grad_up)


MESH = pl.DeviceIdType.MESH
TILE = 512


def place():
    t = lax.axis_index("tensor")
    c = lax.axis_index("dp")
    z = t // 2
    x = t % 2
    q = z + c * (3 - 2 * z)
    step = 2 * (1 - 2 * c)
    first = jnp.minimum(q, 1)
    return t, c, x, q, {"tensor": t + 1 - 2 * x}, {"tensor": t + step}, {"tensor": t - step}, {"dp": 1 - c}, first


def greet(q, xn, up, dn, sib):
    barrier = pltpu.get_barrier_semaphore()
    pl.semaphore_signal(barrier, inc=1, device_id=xn, device_id_type=MESH)
    pl.semaphore_signal(barrier, inc=1, device_id=sib, device_id_type=MESH)

    @pl.when(q < 3)
    def _():
        pl.semaphore_signal(barrier, inc=1, device_id=up, device_id_type=MESH)

    @pl.when(q > 0)
    def _():
        pl.semaphore_signal(barrier, inc=1, device_id=dn, device_id_type=MESH)

    ends = (q == 0) | (q == 3)

    @pl.when(ends)
    def _():
        pl.semaphore_wait(barrier, 3)

    @pl.when(jnp.logical_not(ends))
    def _():
        pl.semaphore_wait(barrier, 4)


def remote(src, dst, send, recv, to):
    return pltpu.make_async_remote_copy(
        src_ref=src, dst_ref=dst, send_sem=send, recv_sem=recv, device_id=to, device_id_type=MESH
    )


def masked(w, m):
    blocks, width = m.shape
    wide = jnp.broadcast_to(m[:, None, :], (blocks, 16, width)).astype(jnp.bfloat16)
    out = w.reshape(blocks, BLOCK // 16, 16, width) * wide[:, None]
    return out.reshape(blocks * BLOCK, width)


def forward_kernel(
    tok_ref, wg_ref, wu_ref, mg_ref, mu_ref, cot_ref,
    hid_ref, xt_ref, d_ref,
    xbuf, wbuf, acc, rbuf, dbuf,
    w_sem, sib_send, x_send, up_send, dn_send, own_recv, x_recv, a_send, a_recv, d_send, d_recv,
):
    t, c, x, q, xn, up, dn, sib, f = place()
    s = 1 - f
    kk = xbuf.shape[-1]
    per = kk // BLOCK
    tiles = acc.shape[0]

    def slot(qs, o):
        return ((qs + c * (1 - 2 * qs)) * 2 + (x + o * (1 - 2 * x)))

    order = ((f, 0), (f, 1), (s, 0), (s, 1))

    def weight_copy(i, gu):
        qs, o = order[i]
        src = (wg_ref, wu_ref)[gu]
        rows = pl.ds(pl.multiple_of(slot(qs, o) * kk, kk), kk)
        return pltpu.make_async_copy(src.at[rows, :], wbuf.at[gu, i], w_sem.at[gu, i])

    for i in range(4):
        for gu in range(2):
            weight_copy(i, gu).start()

    greet(q, xn, up, dn, sib)

    @pl.when(q >= 2)
    def _():
        remote(tok_ref, xbuf.at[jnp.minimum(3 - q, 1), 0, 1], sib_send, own_recv.at[jnp.minimum(3 - q, 1), 1], sib).start()

    @pl.when(q < 2)
    def _():
        xbuf[f, 0, 0] = tok_ref[...]

    def x_copy(qs, h):
        return remote(xbuf.at[qs, 0, h], xbuf.at[qs, 1, h], x_send.at[qs, h], x_recv.at[qs, h], xn)

    def up_copy(qs, h):
        return remote(xbuf.at[qs, 0, h], xbuf.at[qs, 0, h], up_send.at[qs, h], own_recv.at[qs, h], up)

    def dn_copy(qs, h):
        return remote(xbuf.at[qs, 0, h], xbuf.at[qs, 0, h], dn_send.at[h], own_recv.at[qs, h], dn)

    def send_first(qs, h):
        x_copy(qs, h).start()

        @pl.when(q < 3)
        def _():
            up_copy(qs, h).start()

        @pl.when(q == 1)
        def _():
            dn_copy(qs, h).start()

    @pl.when(q >= 2)
    def _():
        up_copy(f, 0).wait_recv()

    send_first(f, 0)
    up_copy(f, 1).wait_recv()
    send_first(f, 1)

    def second(h):
        up_copy(s, h).wait_recv()
        x_copy(s, h).start()

        @pl.when((q == 1) | (q == 2))
        def _():
            up_copy(s, h).start()

    def block(i):
        qs, o = order[i]
        at = slot(qs, o)
        if o == 1:
            x_copy(qs, 0).wait_recv()
            x_copy(qs, 1).wait_recv()
        rows = pl.ds(pl.multiple_of(at * kk, kk), kk)
        for h in range(2):
            xt_ref[rows, pl.ds(h * xbuf.shape[3], xbuf.shape[3])] = xbuf[qs, o, h].T
        weight_copy(i, 0).wait()
        weight_copy(i, 1).wait()

        def tile(j, _):
            cols = pl.ds(pl.multiple_of(j * TILE, TILE), TILE)
            xs = xbuf[qs, o].reshape(-1, kk)
            for gu, m_ref in ((0, mg_ref), (1, mu_ref)):
                m = m_ref[pl.ds(pl.multiple_of(at * per, per), per), cols]
                w = masked(wbuf[gu, i, :, cols], m)
                y = jnp.dot(xs, w, preferred_element_type=jnp.float32)
                half = y.shape[0] // 2
                if i == 0:
                    acc[j, 0, gu] = y[:half]
                    acc[j, 1, gu] = y[half:]
                else:
                    acc[j, 0, gu] += y[:half]
                    acc[j, 1, gu] += y[half:]
            if i == 3:
                remote(acc.at[j, 1], rbuf.at[j], a_send.at[j], a_recv.at[j], sib).start()
            return 0

        lax.fori_loop(0, tiles, tile, 0)

    block(0)
    second(0)
    second(1)
    block(1)
    block(2)
    block(3)

    def point(j, _):
        cols = pl.ds(pl.multiple_of(j * TILE, TILE), TILE)
        remote(acc.at[j, 1], rbuf.at[j], a_send.at[j], a_recv.at[j], sib).wait_recv()
        gate = acc[j, 0, 0] + rbuf[j, 0]
        upv = acc[j, 0, 1] + rbuf[j, 1]
        sig = jax.nn.sigmoid(gate)
        act = gate * sig
        hid_ref[:, cols] = (act * upv).astype(jnp.bfloat16)
        g = cot_ref[:, cols].astype(jnp.float32)
        dg = (g * upv * sig * (1.0 + gate * (1.0 - sig))).astype(jnp.bfloat16)
        du = (g * act).astype(jnp.bfloat16)
        dbuf[j, 0, 0] = dg
        dbuf[j, 0, 1] = du
        remote(dbuf.at[j, 0], dbuf.at[j, 1], d_send.at[j], d_recv.at[j], sib).start()
        d_ref[0, 0, :, cols] = dg
        d_ref[1, 0, :, cols] = du
        return 0

    lax.fori_loop(0, tiles, point, 0)

    def collect(j, _):
        cols = pl.ds(pl.multiple_of(j * TILE, TILE), TILE)
        remote(dbuf.at[j, 0], dbuf.at[j, 1], d_send.at[j], d_recv.at[j], sib).wait()
        d_ref[0, 1, :, cols] = dbuf[j, 1, 0]
        d_ref[1, 1, :, cols] = dbuf[j, 1, 1]
        remote(acc.at[j, 1], rbuf.at[j], a_send.at[j], a_recv.at[j], sib).wait_send()
        return 0

    lax.fori_loop(0, tiles, collect, 0)

    for h in range(2):
        x_copy(f, h).wait_send()
        x_copy(s, h).wait_send()

        @pl.when(q < 3)
        def _():
            up_copy(f, h).wait_send()

        @pl.when((q == 1) | (q == 2))
        def _():
            up_copy(s, h).wait_send()

        @pl.when(q == 1)
        def _():
            dn_copy(f, h).wait_send()

    @pl.when(q >= 2)
    def _():
        remote(tok_ref, xbuf.at[jnp.minimum(3 - q, 1), 0, 1], sib_send, own_recv.at[jnp.minimum(3 - q, 1), 1], sib).wait_send()


def input_kernel(
    d_ref, wg_ref, wu_ref, mg_ref, mu_ref,
    out_ref,
    wbuf, psum, xout, xin, zout, upin, dnin, fout, fin,
    w_sem, x_send, x_recv, z_send, up_recv, dn_recv, f_send, f_recv,
):
    t, c, x, q, xn, up, dn, sib, f = place()
    s = 1 - f
    kk = psum.shape[-1]
    per = kk // BLOCK

    def slot(qs, o):
        return ((qs + c * (1 - 2 * qs)) * 2 + (x + o * (1 - 2 * x)))

    order = ((s, 1), (f, 1), (s, 0), (f, 0))

    def weight_copy(i, gu):
        qs, o = order[i]
        src = (wg_ref, wu_ref)[gu]
        rows = pl.ds(pl.multiple_of(slot(qs, o) * kk, kk), kk)
        return pltpu.make_async_copy(src.at[rows, :], wbuf.at[gu, i], w_sem.at[gu, i])

    for i in range(4):
        for gu in range(2):
            weight_copy(i, gu).start()

    greet(q, xn, up, dn, sib)
    part = 256
    steps = kk // part

    def block(i):
        qs, o = order[i]
        at = slot(qs, o)
        weight_copy(i, 0).wait()
        weight_copy(i, 1).wait()

        def tile(j, _):
            rows = pl.ds(pl.multiple_of(j * part, part), part)
            total = None
            for gu, m_ref in ((0, mg_ref), (1, mu_ref)):
                wide = []
                for b in range(part // BLOCK):
                    m = m_ref[pl.ds(at * per + j * (part // BLOCK) + b, 1), :]
                    mm = jnp.broadcast_to(m, (16, m.shape[1])).astype(jnp.bfloat16)
                    w = wbuf[gu, i, pl.ds(pl.multiple_of(j * part + b * BLOCK, BLOCK), BLOCK), :]
                    wide.append((w.reshape(BLOCK // 16, 16, -1) * mm[None]).reshape(BLOCK, -1))
                w = jnp.concatenate(wide, axis=0)
                y = lax.dot_general(
                    d_ref[gu].reshape(-1, w.shape[1]), w, (((1,), (1,)), ((), ())),
                    preferred_element_type=jnp.float32,
                )
                total = y if total is None else total + y
            half = total.shape[0] // 2
            for h in range(2):
                value = total[h * half:(h + 1) * half]
                if o == 1:
                    xout[i, h, :, rows] = value.astype(jnp.bfloat16)
                else:
                    psum[i - 2, h, :, rows] = value
            return 0

        lax.fori_loop(0, steps, tile, 0)

    def x_copy(k, h):
        return remote(xout.at[k, h], xin.at[k, h], x_send.at[k, h], x_recv.at[k, h], xn)

    def z_copy(k, h, to, dst, sem):
        return remote(zout.at[k, h], dst, z_send.at[k, h], sem, to)

    for k in range(2):
        block(k)
        for h in range(2):
            x_copy(k, h).start()
    block(2)
    block(3)

    for h in range(2):
        x_copy(0, h).wait_recv()

        @pl.when((q == 1) | (q == 2))
        def _():
            z_copy(0, h, dn, upin.at[s, h], up_recv.at[s, h]).wait_recv()
            zout[0, h] = (psum[0, h] + xin[0, h].astype(jnp.float32) + upin[s, h].astype(jnp.float32)).astype(jnp.bfloat16)

        @pl.when((q == 0) | (q == 3))
        def _():
            zout[0, h] = (psum[0, h] + xin[0, h].astype(jnp.float32)).astype(jnp.bfloat16)

        @pl.when(q == 0)
        def _():
            z_copy(0, h, up, dnin.at[h], dn_recv.at[h]).start()

        @pl.when(q > 0)
        def _():
            z_copy(0, h, dn, upin.at[s, h], up_recv.at[s, h]).start()

    def final_copy():
        return remote(fout, fin, f_send, f_recv, sib)

    for h in (1, 0):
        x_copy(1, h).wait_recv()
        psum[1, h] += xin[1, h].astype(jnp.float32)

        @pl.when(q < 3)
        def _():
            z_copy(1, h, dn, upin.at[f, h], up_recv.at[f, h]).wait_recv()
            psum[1, h] += upin[f, h].astype(jnp.float32)

        @pl.when(q == 1)
        def _():
            z_copy(0, h, up, dnin.at[h], dn_recv.at[h]).wait_recv()
            psum[1, h] += dnin[h].astype(jnp.float32)

        @pl.when(q >= 2)
        def _():
            zout[1, h] = psum[1, h].astype(jnp.bfloat16)
            z_copy(1, h, dn, upin.at[f, h], up_recv.at[f, h]).start()

        @pl.when(q < 2)
        def _():
            if h == 1:
                fout[...] = psum[1, h].astype(jnp.bfloat16)
                final_copy().start()
            else:
                out_ref[...] = psum[1, h].astype(jnp.bfloat16)

    @pl.when(q >= 2)
    def _():
        final_copy().wait_recv()
        out_ref[...] = fin[...]

    @pl.when(q < 2)
    def _():
        final_copy().wait_send()

    for h in range(2):
        x_copy(0, h).wait_send()
        x_copy(1, h).wait_send()
        z_copy(0, h, dn, upin.at[s, h], up_recv.at[s, h]).wait_send()

        @pl.when(q >= 2)
        def _():
            z_copy(1, h, dn, upin.at[f, h], up_recv.at[f, h]).wait_send()


def weight_kernel(xt_ref, d_ref, mg_ref, mu_ref, gg_ref, gu_ref):
    width = gg_ref.shape[1]
    for j in range(width // TILE):
        cols = pl.ds(j * TILE, TILE)
        for gu, m_ref, o_ref in ((0, mg_ref, gg_ref), (1, mu_ref, gu_ref)):
            y = jnp.dot(xt_ref[...], d_ref[gu, :, cols], preferred_element_type=jnp.float32)
            o_ref[:, cols] = masked(y.astype(jnp.bfloat16), m_ref[:, cols])


def spread_columns(mask):
    cols = mask.shape[1]
    width = cols * BLOCK
    col_ids = lax.broadcasted_iota(jnp.int32, (cols, width), 1) // BLOCK
    own_ids = lax.broadcasted_iota(jnp.int32, (cols, width), 0)
    spread = (col_ids == own_ids).astype(jnp.bfloat16)
    return jnp.dot(mask.astype(jnp.bfloat16), spread, preferred_element_type=jnp.float32)


def kernel_shards(tokens, gate_weight, up_weight, gate_mask, up_mask, cotangent):
    half, kk = tokens.shape
    rows, width = gate_weight.shape
    tiles = width // TILE
    bf, f32 = jnp.bfloat16, jnp.float32
    mg, mu = spread_columns(gate_mask), spread_columns(up_mask)
    vmem = pl.BlockSpec(memory_space=pltpu.VMEM)
    anyspec = pl.BlockSpec(memory_space=pl.ANY)
    dma = pltpu.SemaphoreType.DMA
    flops = 2 * 2 * 2 * half * rows * width
    cost = pl.CostEstimate(flops=flops, bytes_accessed=4 * rows * width, transcendentals=half * width)
    hidden, xt, d = pl.pallas_call(
        forward_kernel,
        out_shape=(
            jax.ShapeDtypeStruct((half, width), bf),
            jax.ShapeDtypeStruct((rows, 2 * half), bf),
            jax.ShapeDtypeStruct((2, 2, half, width), bf),
        ),
        in_specs=[vmem, anyspec, anyspec, vmem, vmem, vmem],
        out_specs=(vmem, vmem, vmem),
        scratch_shapes=[
            pltpu.VMEM((2, 2, 2, half, kk), bf),
            pltpu.VMEM((2, 4, kk, width), bf),
            pltpu.VMEM((tiles, 2, 2, half, TILE), f32),
            pltpu.VMEM((tiles, 2, half, TILE), f32),
            pltpu.VMEM((tiles, 2, 2, half, TILE), bf),
            dma((2, 4)), dma, dma((2, 2)), dma((2, 2)), dma((2,)), dma((2, 2)), dma((2, 2)),
            dma((tiles,)), dma((tiles,)), dma((tiles,)), dma((tiles,)),
        ],
        compiler_params=pltpu.CompilerParams(
            collective_id=0, has_side_effects=True, vmem_limit_bytes=60 * 2**20
        ),
        cost_estimate=cost,
    )(tokens, gate_weight, up_weight, mg, mu, cotangent)
    block = (2, half, kk)
    grad_input = pl.pallas_call(
        input_kernel,
        out_shape=jax.ShapeDtypeStruct((half, kk), bf),
        in_specs=[vmem, anyspec, anyspec, vmem, vmem],
        out_specs=vmem,
        scratch_shapes=[
            pltpu.VMEM((2, 4, kk, width), bf),
            pltpu.VMEM((2,) + block, f32),
            pltpu.VMEM((2,) + block, bf),
            pltpu.VMEM((2,) + block, bf),
            pltpu.VMEM((2,) + block, bf),
            pltpu.VMEM((2,) + block, bf),
            pltpu.VMEM(block, bf),
            pltpu.VMEM((half, kk), bf),
            pltpu.VMEM((half, kk), bf),
            dma((2, 4)), dma((2, 2)), dma((2, 2)), dma((2, 2)), dma((2, 2)), dma((2,)), dma, dma,
        ],
        compiler_params=pltpu.CompilerParams(
            collective_id=1, has_side_effects=True, vmem_limit_bytes=60 * 2**20
        ),
        cost_estimate=cost,
    )(d, gate_weight, up_weight, mg, mu)
    step = 512
    d_all = d.reshape(2, 2 * half, width)
    mask_spec = pl.BlockSpec((step // BLOCK, width), lambda i: (i, 0))
    out_spec = pl.BlockSpec((step, width), lambda i: (i, 0))
    grad_gate, grad_up = pl.pallas_call(
        weight_kernel,
        grid=(rows // step,),
        out_shape=(jax.ShapeDtypeStruct((rows, width), bf),) * 2,
        in_specs=[
            pl.BlockSpec((step, 2 * half), lambda i: (i, 0)),
            pl.BlockSpec((2, 2 * half, width), lambda i: (0, 0, 0)),
            mask_spec,
            mask_spec,
        ],
        out_specs=(out_spec, out_spec),
        compiler_params=pltpu.CompilerParams(vmem_limit_bytes=48 * 2**20),
        cost_estimate=cost,
    )(xt, d_all, mg, mu)
    return (hidden, grad_input, grad_gate, grad_up)


def body(mesh):
    return kernel_shards if mesh.shape["tensor"] == 8 and mesh.shape["dp"] == 2 else shards


def solution(mesh):
    in_specs = (
        P(("groups", "dp"), "tensor"),
        P("dp", "tensor"),
        P("dp", "tensor"),
        P("dp", "tensor"),
        P("dp", "tensor"),
        P(("groups", "dp"), "tensor"),
    )
    out_specs = (
        P(("groups", "dp"), "tensor"),
        P(("groups", "dp"), "tensor"),
        P("dp", ("groups", "tensor")),
        P("dp", ("groups", "tensor")),
    )
    return jax.shard_map(body(mesh), mesh=mesh, in_specs=in_specs, out_specs=out_specs, check_vma=False)
```

```python
import jax
import jax.numpy as jnp
from jax import lax
from jax.experimental import pallas as pl
from jax.experimental.pallas import tpu as pltpu
from jax.sharding import PartitionSpec as P

BLOCK = 64


def expand_blocks(mask):
    rows, cols = mask.shape
    width = cols * BLOCK
    col_ids = lax.broadcasted_iota(jnp.int32, (cols, width), 1) // BLOCK
    own_ids = lax.broadcasted_iota(jnp.int32, (cols, width), 0)
    spread = (col_ids == own_ids).astype(jnp.bfloat16)
    wide_cols = jnp.dot(
        mask.astype(jnp.bfloat16), spread, preferred_element_type=jnp.float32
    ).astype(jnp.bfloat16)
    wide = jnp.broadcast_to(wide_cols[:, None, :], (rows, BLOCK, width))
    return wide.reshape(rows * BLOCK, width)


def shards(tokens, gate_weight, up_weight, gate_mask, up_mask, cotangent):
    gate_wide = expand_blocks(gate_mask)
    up_wide = expand_blocks(up_mask)
    gate_kept = gate_weight * gate_wide
    up_kept = up_weight * up_wide
    own_rows = lax.all_gather(tokens, "tensor", axis=1, tiled=True)
    half_block = lax.all_to_all(own_rows, "dp", split_axis=1, concat_axis=0, tiled=True)
    gate_full, up_full = (
        lax.all_gather(gate_kept, "dp", axis=0, tiled=True),
        lax.all_gather(up_kept, "dp", axis=0, tiled=True),
    )
    gate = jnp.dot(own_rows, gate_full, preferred_element_type=jnp.float32)
    up = jnp.dot(own_rows, up_full, preferred_element_type=jnp.float32)
    sig = jax.nn.sigmoid(gate)
    act = gate * sig
    hidden = (act * up).astype(jnp.bfloat16)
    grad_out = cotangent.astype(jnp.float32)
    d_gate = (grad_out * up * sig * (1.0 + gate * (1.0 - sig))).astype(jnp.bfloat16)
    d_up = (grad_out * act).astype(jnp.bfloat16)
    gate_all, up_all = (
        lax.all_gather(d_gate, "dp", axis=0, tiled=True),
        lax.all_gather(d_up, "dp", axis=0, tiled=True),
    )
    total = jnp.einsum("dh,th->dt", gate_full, d_gate, preferred_element_type=jnp.float32)
    input_terms = lax.psum_scatter(
        total + jnp.einsum("dh,th->dt", up_full, d_up, preferred_element_type=jnp.float32),
        "tensor",
        scatter_dimension=0,
        tiled=True,
    )
    grad_input = input_terms.T.astype(jnp.bfloat16)
    grad_gate = jnp.einsum("td,th->dh", half_block, gate_all, preferred_element_type=jnp.float32)
    grad_up = jnp.einsum("td,th->dh", half_block, up_all, preferred_element_type=jnp.float32)
    grad_gate = (grad_gate * gate_wide.astype(jnp.float32)).astype(jnp.bfloat16)
    grad_up = (grad_up * up_wide.astype(jnp.float32)).astype(jnp.bfloat16)
    return (hidden, grad_input, grad_gate, grad_up)


MESH = pl.DeviceIdType.MESH
TILE = 512


def place():
    t = lax.axis_index("tensor")
    c = lax.axis_index("dp")
    z = t // 2
    x = t % 2
    q = z + c * (3 - 2 * z)
    step = 2 * (1 - 2 * c)
    first = jnp.minimum(q, 1)
    return t, c, x, q, {"tensor": t + 1 - 2 * x}, {"tensor": t + step}, {"tensor": t - step}, {"dp": 1 - c}, first


def greet(q, xn, up, dn, sib):
    barrier = pltpu.get_barrier_semaphore()
    pl.semaphore_signal(barrier, inc=1, device_id=xn, device_id_type=MESH)
    pl.semaphore_signal(barrier, inc=1, device_id=sib, device_id_type=MESH)

    @pl.when(q < 3)
    def _():
        pl.semaphore_signal(barrier, inc=1, device_id=up, device_id_type=MESH)

    @pl.when(q > 0)
    def _():
        pl.semaphore_signal(barrier, inc=1, device_id=dn, device_id_type=MESH)

    ends = (q == 0) | (q == 3)

    @pl.when(ends)
    def _():
        pl.semaphore_wait(barrier, 3)

    @pl.when(jnp.logical_not(ends))
    def _():
        pl.semaphore_wait(barrier, 4)


def remote(src, dst, send, recv, to):
    return pltpu.make_async_remote_copy(
        src_ref=src, dst_ref=dst, send_sem=send, recv_sem=recv, device_id=to, device_id_type=MESH
    )


def masked(w, m):
    blocks, width = m.shape
    wide = jnp.broadcast_to(m[:, None, :], (blocks, 16, width)).astype(jnp.bfloat16)
    out = w.reshape(blocks, BLOCK // 16, 16, width) * wide[:, None]
    return out.reshape(blocks * BLOCK, width)


def main_kernel(
    tok_ref, wg_ref, wu_ref, mg_ref, mu_ref, cot_ref,
    hid_ref, xt_ref, d_ref, out_ref,
    xbuf, wbuf, mwide, acc, rbuf, dbuf, psum, xout, xin, zout, upin, dnin, fout, fin,
    w_sem, sib_send, x_send, up_send, dn_send, own_recv, x_recv, a_send, a_recv, d_send, d_recv,
    r_send, r_recv, z_send, z_recv, n_recv, f_send, f_recv,
):
    t, c, x, q, xn, up, dn, sib, f = place()
    s = 1 - f
    kk = xbuf.shape[-1]
    per = kk // BLOCK
    tiles = acc.shape[0]

    def slot(qs, o):
        return ((qs + c * (1 - 2 * qs)) * 2 + (x + o * (1 - 2 * x)))

    order = ((f, 0), (f, 1), (s, 0), (s, 1))

    def weight_copy(i, gu):
        qs, o = order[i]
        src = (wg_ref, wu_ref)[gu]
        rows = pl.ds(pl.multiple_of(slot(qs, o) * kk, kk), kk)
        return pltpu.make_async_copy(src.at[rows, :], wbuf.at[gu, i], w_sem.at[gu, i])

    for i in range(2):
        for gu in range(2):
            weight_copy(i, gu).start()

    greet(q, xn, up, dn, sib)

    @pl.when(q >= 2)
    def _():
        remote(tok_ref, xbuf.at[jnp.minimum(3 - q, 1), 0, 1], sib_send, own_recv.at[jnp.minimum(3 - q, 1), 1], sib).start()

    @pl.when(q < 2)
    def _():
        xbuf[f, 0, 0] = tok_ref[...]

    def x_copy(qs, h):
        return remote(xbuf.at[qs, 0, h], xbuf.at[qs, 1, h], x_send.at[qs, h], x_recv.at[qs, h], xn)

    def up_copy(qs, h):
        return remote(xbuf.at[qs, 0, h], xbuf.at[qs, 0, h], up_send.at[qs, h], own_recv.at[qs, h], up)

    def dn_copy(qs, h):
        return remote(xbuf.at[qs, 0, h], xbuf.at[qs, 0, h], dn_send.at[h], own_recv.at[qs, h], dn)

    def send_first(qs, h):
        x_copy(qs, h).start()

        @pl.when(q < 3)
        def _():
            up_copy(qs, h).start()

        @pl.when(q == 1)
        def _():
            dn_copy(qs, h).start()

    @pl.when(q >= 2)
    def _():
        up_copy(f, 0).wait_recv()

    send_first(f, 0)
    up_copy(f, 1).wait_recv()
    send_first(f, 1)
    for i in range(2, 4):
        for gu in range(2):
            weight_copy(i, gu).start()

    mwide[0] = spread_columns(mg_ref[...])
    mwide[1] = spread_columns(mu_ref[...])

    def mask_block(i):
        qs, o = order[i]
        at = slot(qs, o)
        weight_copy(i, 0).wait()
        weight_copy(i, 1).wait()

        def strip(b, _):
            rows = pl.ds(pl.multiple_of(b * BLOCK, BLOCK), BLOCK)
            for gu in range(2):
                m = mwide[gu, pl.ds(at * per + b, 1), :]
                wide = jnp.broadcast_to(m, (16, m.shape[1])).astype(jnp.bfloat16)
                w = wbuf[gu, i, rows, :].reshape(BLOCK // 16, 16, m.shape[1])
                wbuf[gu, i, rows, :] = (w * wide[None]).reshape(BLOCK, m.shape[1])
            return 0

        lax.fori_loop(0, per, strip, 0)

    def second(h):
        up_copy(s, h).wait_recv()
        x_copy(s, h).start()

        @pl.when((q == 1) | (q == 2))
        def _():
            up_copy(s, h).start()

    def block(i):
        qs, o = order[i]
        at = slot(qs, o)
        if o == 1:
            x_copy(qs, 0).wait_recv()
            x_copy(qs, 1).wait_recv()
        rows = pl.ds(pl.multiple_of(at * kk, kk), kk)
        for h in range(2):
            xt_ref[rows, pl.ds(h * xbuf.shape[3], xbuf.shape[3])] = xbuf[qs, o, h].T

        def tile(j, _):
            cols = pl.ds(pl.multiple_of(j * TILE, TILE), TILE)
            xs = xbuf[qs, o].reshape(-1, kk)
            for gu in range(2):
                y = jnp.dot(xs, wbuf[gu, i, :, cols], preferred_element_type=jnp.float32)
                half = y.shape[0] // 2
                if i == 0:
                    acc[j, 0, gu] = y[:half]
                    acc[j, 1, gu] = y[half:]
                else:
                    acc[j, 0, gu] += y[:half]
                    acc[j, 1, gu] += y[half:]
            if i == 3:
                remote(acc.at[j, 1], rbuf.at[j], a_send.at[j], a_recv.at[j], sib).start()
            return 0

        lax.fori_loop(0, tiles, tile, 0)

    mask_block(0)
    second(0)
    mask_block(1)
    second(1)
    block(0)
    mask_block(2)
    block(1)
    mask_block(3)
    block(2)
    block(3)

    def point(j, _):
        cols = pl.ds(pl.multiple_of(j * TILE, TILE), TILE)
        remote(acc.at[j, 1], rbuf.at[j], a_send.at[j], a_recv.at[j], sib).wait_recv()
        gate = acc[j, 0, 0] + rbuf[j, 0]
        upv = acc[j, 0, 1] + rbuf[j, 1]
        sig = jax.nn.sigmoid(gate)
        act = gate * sig
        hid_ref[:, cols] = (act * upv).astype(jnp.bfloat16)
        g = cot_ref[:, cols].astype(jnp.float32)
        dg = (g * upv * sig * (1.0 + gate * (1.0 - sig))).astype(jnp.bfloat16)
        du = (g * act).astype(jnp.bfloat16)
        dbuf[j, 0, 0] = dg
        dbuf[j, 0, 1] = du
        remote(dbuf.at[j, 0], dbuf.at[j, 1], d_send.at[j], d_recv.at[j], sib).start()
        d_ref[0, 0, :, cols] = dg
        d_ref[1, 0, :, cols] = du
        return 0

    lax.fori_loop(0, tiles, point, 0)

    def collect(j, _):
        cols = pl.ds(pl.multiple_of(j * TILE, TILE), TILE)
        remote(dbuf.at[j, 0], dbuf.at[j, 1], d_send.at[j], d_recv.at[j], sib).wait()
        d_ref[0, 1, :, cols] = dbuf[j, 1, 0]
        d_ref[1, 1, :, cols] = dbuf[j, 1, 1]
        remote(acc.at[j, 1], rbuf.at[j], a_send.at[j], a_recv.at[j], sib).wait_send()
        return 0

    lax.fori_loop(0, tiles, collect, 0)

    steps, part = xout.shape[1], xout.shape[3]
    half = xout.shape[2] // 2

    def r_copy(k, j):
        return remote(xout.at[k, j], xin.at[k, j], r_send.at[k, j], r_recv.at[k, j], xn)

    def z_copy(k, j):
        qs = (s, f)[k]
        return remote(zout.at[k, j], upin.at[qs, j], z_send.at[k, j], z_recv.at[qs, j], dn)

    def n_copy(j):
        return remote(zout.at[0, j], dnin.at[j], z_send.at[0, j], n_recv.at[j], up)

    def f_copy(j):
        return remote(fout.at[j], fin.at[j], f_send.at[j], f_recv.at[j], sib)

    def partial(i, k, away):
        def tile(j, _):
            rows = pl.ds(pl.multiple_of(j * part, part), part)
            total = None
            for gu in range(2):
                w = wbuf[gu, i, rows, :]
                y = lax.dot_general(
                    d_ref[gu].reshape(-1, w.shape[1]), w, (((1,), (1,)), ((), ())),
                    preferred_element_type=jnp.float32,
                )
                total = y if total is None else total + y
            if away:
                xout[k, j] = total.astype(jnp.bfloat16)
                r_copy(k, j).start()
            else:
                psum[k, j] = total
            return 0

        lax.fori_loop(0, steps, tile, 0)

    partial(3, 0, True)
    partial(1, 1, True)
    partial(2, 0, False)
    partial(0, 1, False)

    def hop(j, _):
        r_copy(0, j).wait_recv()
        psum[0, j] += xin[0, j].astype(jnp.float32)

        @pl.when((q == 1) | (q == 2))
        def _():
            z_copy(0, j).wait_recv()
            psum[0, j] += upin[s, j].astype(jnp.float32)

        zout[0, j] = psum[0, j].astype(jnp.bfloat16)

        @pl.when(q == 0)
        def _():
            n_copy(j).start()

        @pl.when(q > 0)
        def _():
            z_copy(0, j).start()

        return 0

    lax.fori_loop(0, steps, hop, 0)

    def last(j, _):
        r_copy(1, j).wait_recv()
        psum[1, j] += xin[1, j].astype(jnp.float32)

        @pl.when(q < 3)
        def _():
            z_copy(1, j).wait_recv()
            psum[1, j] += upin[f, j].astype(jnp.float32)

        @pl.when(q == 1)
        def _():
            n_copy(j).wait_recv()
            psum[1, j] += dnin[j].astype(jnp.float32)

        @pl.when(q >= 2)
        def _():
            zout[1, j] = psum[1, j].astype(jnp.bfloat16)
            z_copy(1, j).start()

        @pl.when(q < 2)
        def _():
            fout[j] = psum[1, j, half:].astype(jnp.bfloat16)
            f_copy(j).start()
            out_ref[:, pl.ds(pl.multiple_of(j * part, part), part)] = psum[1, j, :half].astype(jnp.bfloat16)

        return 0

    lax.fori_loop(0, steps, last, 0)

    def finish(j, _):
        @pl.when(q >= 2)
        def _():
            f_copy(j).wait_recv()
            out_ref[:, pl.ds(pl.multiple_of(j * part, part), part)] = fin[j]
            z_copy(1, j).wait_send()

        @pl.when(q < 2)
        def _():
            f_copy(j).wait_send()

        r_copy(0, j).wait_send()
        r_copy(1, j).wait_send()
        z_copy(0, j).wait_send()
        return 0

    lax.fori_loop(0, steps, finish, 0)

    for h in range(2):
        x_copy(f, h).wait_send()
        x_copy(s, h).wait_send()

        @pl.when(q < 3)
        def _():
            up_copy(f, h).wait_send()

        @pl.when((q == 1) | (q == 2))
        def _():
            up_copy(s, h).wait_send()

        @pl.when(q == 1)
        def _():
            dn_copy(f, h).wait_send()

    @pl.when(q >= 2)
    def _():
        remote(tok_ref, xbuf.at[jnp.minimum(3 - q, 1), 0, 1], sib_send, own_recv.at[jnp.minimum(3 - q, 1), 1], sib).wait_send()


def weight_kernel(xt_ref, d_ref, mg_ref, mu_ref, hid_ref, in_ref, gg_ref, gu_ref, hid_out, in_out, mwide):
    i = pl.program_id(0)
    per = xt_ref.shape[0] // BLOCK

    @pl.when(i == 0)
    def _():
        mwide[0] = spread_columns(mg_ref[...])
        mwide[1] = spread_columns(mu_ref[...])

    hid_out[...] = hid_ref[...]
    in_out[...] = in_ref[...]
    width = gg_ref.shape[1]
    for j in range(width // TILE):
        cols = pl.ds(j * TILE, TILE)
        for gu, o_ref in ((0, gg_ref), (1, gu_ref)):
            y = jnp.dot(xt_ref[...], d_ref[gu, :, cols], preferred_element_type=jnp.float32)
            m = mwide[gu, pl.ds(pl.multiple_of(i * per, per), per), cols]
            o_ref[:, cols] = masked(y.astype(jnp.bfloat16), m)


def spread_columns(mask):
    cols = mask.shape[1]
    width = cols * BLOCK
    col_ids = lax.broadcasted_iota(jnp.int32, (cols, width), 1) // BLOCK
    own_ids = lax.broadcasted_iota(jnp.int32, (cols, width), 0)
    spread = (col_ids == own_ids).astype(jnp.bfloat16)
    return jnp.dot(mask.astype(jnp.bfloat16), spread, preferred_element_type=jnp.float32)


def kernel_shards(tokens, gate_weight, up_weight, gate_mask, up_mask, cotangent):
    half, kk = tokens.shape
    rows, width = gate_weight.shape
    tiles = width // TILE
    part = 256
    steps = kk // part
    bf, f32 = jnp.bfloat16, jnp.float32
    vmem = pl.BlockSpec(memory_space=pltpu.VMEM)
    anyspec = pl.BlockSpec(memory_space=pl.ANY)
    dma = pltpu.SemaphoreType.DMA
    flops = 2 * 2 * 2 * half * rows * width
    chunks = (steps, 2 * half, part)
    hidden, xt, d, grad_input = pl.pallas_call(
        main_kernel,
        out_shape=(
            jax.ShapeDtypeStruct((half, width), bf),
            jax.ShapeDtypeStruct((rows, 2 * half), bf),
            jax.ShapeDtypeStruct((2, 2, half, width), bf),
            jax.ShapeDtypeStruct((half, kk), bf),
        ),
        in_specs=[vmem, anyspec, anyspec, vmem, vmem, vmem],
        out_specs=(vmem, vmem, vmem, vmem),
        scratch_shapes=[
            pltpu.VMEM((2, 2, 2, half, kk), bf),
            pltpu.VMEM((2, 4, kk, width), bf),
            pltpu.VMEM((2, rows // BLOCK, width), f32),
            pltpu.VMEM((tiles, 2, 2, half, TILE), f32),
            pltpu.VMEM((tiles, 2, half, TILE), f32),
            pltpu.VMEM((tiles, 2, 2, half, TILE), bf),
            pltpu.VMEM((2,) + chunks, f32),
            pltpu.VMEM((2,) + chunks, bf),
            pltpu.VMEM((2,) + chunks, bf),
            pltpu.VMEM((2,) + chunks, bf),
            pltpu.VMEM((2,) + chunks, bf),
            pltpu.VMEM(chunks, bf),
            pltpu.VMEM((steps, half, part), bf),
            pltpu.VMEM((steps, half, part), bf),
            dma((2, 4)), dma, dma((2, 2)), dma((2, 2)), dma((2,)), dma((2, 2)), dma((2, 2)),
            dma((tiles,)), dma((tiles,)), dma((tiles,)), dma((tiles,)),
            dma((2, steps)), dma((2, steps)), dma((2, steps)), dma((2, steps)),
            dma((steps,)), dma((steps,)), dma((steps,)),
        ],
        compiler_params=pltpu.CompilerParams(
            collective_id=0, has_side_effects=True, vmem_limit_bytes=60 * 2**20
        ),
        cost_estimate=pl.CostEstimate(
            flops=2 * flops, bytes_accessed=4 * rows * width, transcendentals=half * width
        ),
    )(tokens, gate_weight, up_weight, gate_mask, up_mask, cotangent)
    step = 512
    grid = rows // step
    mask_spec = pl.BlockSpec(gate_mask.shape, lambda i: (0, 0))
    out_spec = pl.BlockSpec((step, width), lambda i: (i, 0))
    hid_spec = pl.BlockSpec((half // grid, width), lambda i: (i, 0))
    in_spec = pl.BlockSpec((half // grid, kk), lambda i: (i, 0))
    grad_gate, grad_up, hidden, grad_input = pl.pallas_call(
        weight_kernel,
        grid=(grid,),
        out_shape=(
            jax.ShapeDtypeStruct((rows, width), bf),
            jax.ShapeDtypeStruct((rows, width), bf),
            jax.ShapeDtypeStruct((half, width), bf),
            jax.ShapeDtypeStruct((half, kk), bf),
        ),
        in_specs=[
            pl.BlockSpec((step, 2 * half), lambda i: (i, 0)),
            pl.BlockSpec((2, 2 * half, width), lambda i: (0, 0, 0)),
            mask_spec,
            mask_spec,
            hid_spec,
            in_spec,
        ],
        out_specs=(out_spec, out_spec, hid_spec, in_spec),
        scratch_shapes=[pltpu.VMEM((2, rows // BLOCK, width), f32)],
        compiler_params=pltpu.CompilerParams(vmem_limit_bytes=48 * 2**20),
        cost_estimate=pl.CostEstimate(flops=flops, bytes_accessed=4 * rows * width, transcendentals=0),
    )(xt, d.reshape(2, 2 * half, width), gate_mask, up_mask, hidden, grad_input)
    return (hidden, grad_input, grad_gate, grad_up)


def body(mesh):
    return kernel_shards if mesh.shape["tensor"] == 8 and mesh.shape["dp"] == 2 else shards


def solution(mesh):
    in_specs = (
        P(("groups", "dp"), "tensor"),
        P("dp", "tensor"),
        P("dp", "tensor"),
        P("dp", "tensor"),
        P("dp", "tensor"),
        P(("groups", "dp"), "tensor"),
    )
    out_specs = (
        P(("groups", "dp"), "tensor"),
        P(("groups", "dp"), "tensor"),
        P("dp", ("groups", "tensor")),
        P("dp", ("groups", "tensor")),
    )
    return jax.shard_map(body(mesh), mesh=mesh, in_specs=in_specs, out_specs=out_specs, check_vma=False)
```

```python
import jax
import jax.numpy as jnp
from jax import lax
from jax.experimental import pallas as pl
from jax.experimental.pallas import tpu as pltpu
from jax.sharding import PartitionSpec as P

BLOCK = 64


def expand_blocks(mask):
    rows, cols = mask.shape
    width = cols * BLOCK
    col_ids = lax.broadcasted_iota(jnp.int32, (cols, width), 1) // BLOCK
    own_ids = lax.broadcasted_iota(jnp.int32, (cols, width), 0)
    spread = (col_ids == own_ids).astype(jnp.bfloat16)
    wide_cols = jnp.dot(
        mask.astype(jnp.bfloat16), spread, preferred_element_type=jnp.float32
    ).astype(jnp.bfloat16)
    wide = jnp.broadcast_to(wide_cols[:, None, :], (rows, BLOCK, width))
    return wide.reshape(rows * BLOCK, width)


def shards(tokens, gate_weight, up_weight, gate_mask, up_mask, cotangent):
    gate_wide = expand_blocks(gate_mask)
    up_wide = expand_blocks(up_mask)
    gate_kept = gate_weight * gate_wide
    up_kept = up_weight * up_wide
    own_rows = lax.all_gather(tokens, "tensor", axis=1, tiled=True)
    half_block = lax.all_to_all(own_rows, "dp", split_axis=1, concat_axis=0, tiled=True)
    gate_full, up_full = (
        lax.all_gather(gate_kept, "dp", axis=0, tiled=True),
        lax.all_gather(up_kept, "dp", axis=0, tiled=True),
    )
    gate = jnp.dot(own_rows, gate_full, preferred_element_type=jnp.float32)
    up = jnp.dot(own_rows, up_full, preferred_element_type=jnp.float32)
    sig = jax.nn.sigmoid(gate)
    act = gate * sig
    hidden = (act * up).astype(jnp.bfloat16)
    grad_out = cotangent.astype(jnp.float32)
    d_gate = (grad_out * up * sig * (1.0 + gate * (1.0 - sig))).astype(jnp.bfloat16)
    d_up = (grad_out * act).astype(jnp.bfloat16)
    gate_all, up_all = (
        lax.all_gather(d_gate, "dp", axis=0, tiled=True),
        lax.all_gather(d_up, "dp", axis=0, tiled=True),
    )
    total = jnp.einsum("dh,th->dt", gate_full, d_gate, preferred_element_type=jnp.float32)
    input_terms = lax.psum_scatter(
        total + jnp.einsum("dh,th->dt", up_full, d_up, preferred_element_type=jnp.float32),
        "tensor",
        scatter_dimension=0,
        tiled=True,
    )
    grad_input = input_terms.T.astype(jnp.bfloat16)
    grad_gate = jnp.einsum("td,th->dh", half_block, gate_all, preferred_element_type=jnp.float32)
    grad_up = jnp.einsum("td,th->dh", half_block, up_all, preferred_element_type=jnp.float32)
    grad_gate = (grad_gate * gate_wide.astype(jnp.float32)).astype(jnp.bfloat16)
    grad_up = (grad_up * up_wide.astype(jnp.float32)).astype(jnp.bfloat16)
    return (hidden, grad_input, grad_gate, grad_up)


MESH = pl.DeviceIdType.MESH
TILE = 512


def place():
    t = lax.axis_index("tensor")
    c = lax.axis_index("dp")
    z = t // 2
    x = t % 2
    q = z + c * (3 - 2 * z)
    step = 2 * (1 - 2 * c)
    first = jnp.minimum(q, 1)
    return t, c, x, q, {"tensor": t + 1 - 2 * x}, {"tensor": t + step}, {"tensor": t - step}, {"dp": 1 - c}, first


def greet(q, xn, up, dn, sib):
    barrier = pltpu.get_barrier_semaphore()
    pl.semaphore_signal(barrier, inc=1, device_id=xn, device_id_type=MESH)
    pl.semaphore_signal(barrier, inc=1, device_id=sib, device_id_type=MESH)

    @pl.when(q < 3)
    def _():
        pl.semaphore_signal(barrier, inc=1, device_id=up, device_id_type=MESH)

    @pl.when(q > 0)
    def _():
        pl.semaphore_signal(barrier, inc=1, device_id=dn, device_id_type=MESH)

    ends = (q == 0) | (q == 3)

    @pl.when(ends)
    def _():
        pl.semaphore_wait(barrier, 3)

    @pl.when(jnp.logical_not(ends))
    def _():
        pl.semaphore_wait(barrier, 4)


def remote(src, dst, send, recv, to):
    return pltpu.make_async_remote_copy(
        src_ref=src, dst_ref=dst, send_sem=send, recv_sem=recv, device_id=to, device_id_type=MESH
    )


def masked(w, m):
    blocks, width = m.shape
    wide = jnp.broadcast_to(m[:, None, :], (blocks, 16, width)).astype(jnp.bfloat16)
    out = w.reshape(blocks, BLOCK // 16, 16, width) * wide[:, None]
    return out.reshape(blocks * BLOCK, width)


def main_kernel(
    tok_ref, wg_ref, wu_ref, mg_ref, mu_ref, cot_ref,
    hid_ref, xt_ref, d_ref, out_ref,
    xbuf, wbuf, mwide, acc, rbuf, dbuf, psum, xout, xin, zout, upin, dnin, fout, fin,
    w_sem, sib_send, x_send, up_send, dn_send, own_recv, x_recv, a_send, a_recv, d_send, d_recv,
    r_send, r_recv, z_send, z_recv, n_recv, f_send, f_recv,
):
    t, c, x, q, xn, up, dn, sib, f = place()
    s = 1 - f
    kk = xbuf.shape[-1]
    per = kk // BLOCK
    tiles = acc.shape[0]

    def slot(qs, o):
        return ((qs + c * (1 - 2 * qs)) * 2 + (x + o * (1 - 2 * x)))

    order = ((f, 0), (f, 1), (s, 0), (s, 1))

    def weight_copy(i, gu):
        qs, o = order[i]
        src = (wg_ref, wu_ref)[gu]
        rows = pl.ds(pl.multiple_of(slot(qs, o) * kk, kk), kk)
        return pltpu.make_async_copy(src.at[rows, :], wbuf.at[gu, i], w_sem.at[gu, i])

    for i in range(2):
        for gu in range(2):
            weight_copy(i, gu).start()

    greet(q, xn, up, dn, sib)

    @pl.when(q >= 2)
    def _():
        remote(tok_ref, xbuf.at[jnp.minimum(3 - q, 1), 0, 1], sib_send, own_recv.at[jnp.minimum(3 - q, 1), 1], sib).start()

    @pl.when(q < 2)
    def _():
        xbuf[f, 0, 0] = tok_ref[...]

    def x_copy(qs, h):
        return remote(xbuf.at[qs, 0, h], xbuf.at[qs, 1, h], x_send.at[qs, h], x_recv.at[qs, h], xn)

    def up_copy(qs, h):
        return remote(xbuf.at[qs, 0, h], xbuf.at[qs, 0, h], up_send.at[qs, h], own_recv.at[qs, h], up)

    def dn_copy(qs, h):
        return remote(xbuf.at[qs, 0, h], xbuf.at[qs, 0, h], dn_send.at[h], own_recv.at[qs, h], dn)

    def send_first(qs, h):
        x_copy(qs, h).start()

        @pl.when(q < 3)
        def _():
            up_copy(qs, h).start()

        @pl.when(q == 1)
        def _():
            dn_copy(qs, h).start()

    @pl.when(q >= 2)
    def _():
        up_copy(f, 0).wait_recv()

    send_first(f, 0)
    up_copy(f, 1).wait_recv()
    send_first(f, 1)
    for i in range(2, 4):
        for gu in range(2):
            weight_copy(i, gu).start()

    mwide[0] = spread_columns(mg_ref[...])
    mwide[1] = spread_columns(mu_ref[...])

    def mask_block(i):
        qs, o = order[i]
        at = slot(qs, o)
        weight_copy(i, 0).wait()
        weight_copy(i, 1).wait()

        def strip(b, _):
            rows = pl.ds(pl.multiple_of(b * BLOCK, BLOCK), BLOCK)
            for gu in range(2):
                m = mwide[gu, pl.ds(at * per + b, 1), :]
                wide = jnp.broadcast_to(m, (16, m.shape[1])).astype(jnp.bfloat16)
                w = wbuf[gu, i, rows, :].reshape(BLOCK // 16, 16, m.shape[1])
                wbuf[gu, i, rows, :] = (w * wide[None]).reshape(BLOCK, m.shape[1])
            return 0

        lax.fori_loop(0, per, strip, 0)

    def second(h):
        up_copy(s, h).wait_recv()
        x_copy(s, h).start()

        @pl.when((q == 1) | (q == 2))
        def _():
            up_copy(s, h).start()

    def block(i):
        qs, o = order[i]
        at = slot(qs, o)
        if o == 1:
            x_copy(qs, 0).wait_recv()
            x_copy(qs, 1).wait_recv()
        rows = pl.ds(pl.multiple_of(at * kk, kk), kk)
        for h in range(2):
            xt_ref[rows, pl.ds(h * xbuf.shape[3], xbuf.shape[3])] = xbuf[qs, o, h].T

        def tile(j, _):
            cols = pl.ds(pl.multiple_of(j * TILE, TILE), TILE)
            xs = xbuf[qs, o].reshape(-1, kk)
            for gu in range(2):
                y = jnp.dot(xs, wbuf[gu, i, :, cols], preferred_element_type=jnp.float32)
                half = y.shape[0] // 2
                if i == 0:
                    acc[j, 0, gu] = y[:half]
                    acc[j, 1, gu] = y[half:]
                else:
                    acc[j, 0, gu] += y[:half]
                    acc[j, 1, gu] += y[half:]
            if i == 3:
                remote(acc.at[j, 1], rbuf.at[j], a_send.at[j], a_recv.at[j], sib).start()
            return 0

        lax.fori_loop(0, tiles, tile, 0)

    mask_block(0)
    second(0)
    mask_block(1)
    second(1)
    block(0)
    mask_block(2)
    block(1)
    mask_block(3)
    block(2)
    block(3)

    def point(j, _):
        cols = pl.ds(pl.multiple_of(j * TILE, TILE), TILE)
        remote(acc.at[j, 1], rbuf.at[j], a_send.at[j], a_recv.at[j], sib).wait_recv()
        gate = acc[j, 0, 0] + rbuf[j, 0]
        upv = acc[j, 0, 1] + rbuf[j, 1]
        sig = jax.nn.sigmoid(gate)
        act = gate * sig
        hid_ref[:, cols] = (act * upv).astype(jnp.bfloat16)
        g = cot_ref[:, cols].astype(jnp.float32)
        dg = (g * upv * sig * (1.0 + gate * (1.0 - sig))).astype(jnp.bfloat16)
        du = (g * act).astype(jnp.bfloat16)
        dbuf[j, 0, 0] = dg
        dbuf[j, 0, 1] = du
        remote(dbuf.at[j, 0], dbuf.at[j, 1], d_send.at[j], d_recv.at[j], sib).start()
        d_ref[0, 0, :, cols] = dg
        d_ref[1, 0, :, cols] = du
        return 0

    lax.fori_loop(0, tiles, point, 0)

    def collect(j, _):
        cols = pl.ds(pl.multiple_of(j * TILE, TILE), TILE)
        remote(dbuf.at[j, 0], dbuf.at[j, 1], d_send.at[j], d_recv.at[j], sib).wait()
        d_ref[0, 1, :, cols] = dbuf[j, 1, 0]
        d_ref[1, 1, :, cols] = dbuf[j, 1, 1]
        remote(acc.at[j, 1], rbuf.at[j], a_send.at[j], a_recv.at[j], sib).wait_send()
        return 0

    lax.fori_loop(0, tiles, collect, 0)

    steps, part = xout.shape[1], xout.shape[3]
    half = xout.shape[2] // 2

    def r_copy(k, j):
        return remote(xout.at[k, j], xin.at[k, j], r_send.at[k, j], r_recv.at[k, j], xn)

    def z_copy(k, j):
        qs = (s, f)[k]
        return remote(zout.at[k, j], upin.at[qs, j], z_send.at[k, j], z_recv.at[qs, j], dn)

    def n_copy(j):
        return remote(zout.at[0, j], dnin.at[j], z_send.at[0, j], n_recv.at[j], up)

    def f_copy(j):
        return remote(fout.at[j], fin.at[j], f_send.at[j], f_recv.at[j], sib)

    def partial(i, k, away):
        def tile(j, _):
            rows = pl.ds(pl.multiple_of(j * part, part), part)
            total = None
            for gu in range(2):
                w = wbuf[gu, i, rows, :]
                y = lax.dot_general(
                    d_ref[gu].reshape(-1, w.shape[1]), w, (((1,), (1,)), ((), ())),
                    preferred_element_type=jnp.float32,
                )
                total = y if total is None else total + y
            if away:
                xout[k, j] = total.astype(jnp.bfloat16)
                r_copy(k, j).start()
            else:
                psum[k, j] = total
            return 0

        lax.fori_loop(0, steps, tile, 0)

    partial(3, 0, True)
    partial(1, 1, True)
    partial(2, 0, False)
    partial(0, 1, False)

    def hop(j, _):
        r_copy(0, j).wait_recv()
        psum[0, j] += xin[0, j].astype(jnp.float32)

        @pl.when((q == 1) | (q == 2))
        def _():
            z_copy(0, j).wait_recv()
            psum[0, j] += upin[s, j].astype(jnp.float32)

        zout[0, j] = psum[0, j].astype(jnp.bfloat16)

        @pl.when(q == 0)
        def _():
            n_copy(j).start()

        @pl.when(q > 0)
        def _():
            z_copy(0, j).start()

        return 0

    lax.fori_loop(0, steps, hop, 0)

    def last(j, _):
        r_copy(1, j).wait_recv()
        psum[1, j] += xin[1, j].astype(jnp.float32)

        @pl.when(q < 3)
        def _():
            z_copy(1, j).wait_recv()
            psum[1, j] += upin[f, j].astype(jnp.float32)

        @pl.when(q == 1)
        def _():
            n_copy(j).wait_recv()
            psum[1, j] += dnin[j].astype(jnp.float32)

        @pl.when(q >= 2)
        def _():
            zout[1, j] = psum[1, j].astype(jnp.bfloat16)
            z_copy(1, j).start()

        @pl.when(q < 2)
        def _():
            fout[j] = psum[1, j, half:].astype(jnp.bfloat16)
            f_copy(j).start()
            out_ref[:, pl.ds(pl.multiple_of(j * part, part), part)] = psum[1, j, :half].astype(jnp.bfloat16)

        return 0

    lax.fori_loop(0, steps, last, 0)

    def finish(j, _):
        @pl.when(q >= 2)
        def _():
            f_copy(j).wait_recv()
            out_ref[:, pl.ds(pl.multiple_of(j * part, part), part)] = fin[j]
            z_copy(1, j).wait_send()

        @pl.when(q < 2)
        def _():
            f_copy(j).wait_send()

        r_copy(0, j).wait_send()
        r_copy(1, j).wait_send()
        z_copy(0, j).wait_send()
        return 0

    lax.fori_loop(0, steps, finish, 0)

    for h in range(2):
        x_copy(f, h).wait_send()
        x_copy(s, h).wait_send()

        @pl.when(q < 3)
        def _():
            up_copy(f, h).wait_send()

        @pl.when((q == 1) | (q == 2))
        def _():
            up_copy(s, h).wait_send()

        @pl.when(q == 1)
        def _():
            dn_copy(f, h).wait_send()

    @pl.when(q >= 2)
    def _():
        remote(tok_ref, xbuf.at[jnp.minimum(3 - q, 1), 0, 1], sib_send, own_recv.at[jnp.minimum(3 - q, 1), 1], sib).wait_send()


def weight_kernel(xt_ref, d_ref, mg_ref, mu_ref, hid_ref, in_ref, gg_ref, gu_ref, hid_out, in_out, mwide):
    i = pl.program_id(0)
    per = xt_ref.shape[0] // BLOCK

    @pl.when(i == 0)
    def _():
        mwide[0] = spread_columns(mg_ref[...])
        mwide[1] = spread_columns(mu_ref[...])

    hid_out[...] = hid_ref[...]
    in_out[...] = in_ref[...]
    width = gg_ref.shape[1]
    for j in range(width // TILE):
        cols = pl.ds(j * TILE, TILE)
        for gu, o_ref in ((0, gg_ref), (1, gu_ref)):
            y = jnp.dot(xt_ref[...], d_ref[gu, :, cols], preferred_element_type=jnp.float32)
            m = mwide[gu, pl.ds(pl.multiple_of(i * per, per), per), cols]
            o_ref[:, cols] = masked(y.astype(jnp.bfloat16), m)


def spread_columns(mask):
    cols = mask.shape[1]
    width = cols * BLOCK
    col_ids = lax.broadcasted_iota(jnp.int32, (cols, width), 1) // BLOCK
    own_ids = lax.broadcasted_iota(jnp.int32, (cols, width), 0)
    spread = (col_ids == own_ids).astype(jnp.bfloat16)
    return jnp.dot(mask.astype(jnp.bfloat16), spread, preferred_element_type=jnp.float32)


def kernel_shards(tokens, gate_weight, up_weight, gate_mask, up_mask, cotangent):
    half, kk = tokens.shape
    rows, width = gate_weight.shape
    tiles = width // TILE
    part = 256
    steps = kk // part
    bf, f32 = jnp.bfloat16, jnp.float32
    vmem = pl.BlockSpec(memory_space=pltpu.VMEM)
    anyspec = pl.BlockSpec(memory_space=pl.ANY)
    dma = pltpu.SemaphoreType.DMA
    flops = 2 * 2 * 2 * half * rows * width
    chunks = (steps, 2 * half, part)
    hidden, xt, d, grad_input = pl.pallas_call(
        main_kernel,
        out_shape=(
            jax.ShapeDtypeStruct((half, width), bf),
            jax.ShapeDtypeStruct((rows, 2 * half), bf),
            jax.ShapeDtypeStruct((2, 2, half, width), bf),
            jax.ShapeDtypeStruct((half, kk), bf),
        ),
        in_specs=[vmem, anyspec, anyspec, vmem, vmem, vmem],
        out_specs=(vmem, vmem, vmem, vmem),
        scratch_shapes=[
            pltpu.VMEM((2, 2, 2, half, kk), bf),
            pltpu.VMEM((2, 4, kk, width), bf),
            pltpu.VMEM((2, rows // BLOCK, width), f32),
            pltpu.VMEM((tiles, 2, 2, half, TILE), f32),
            pltpu.VMEM((tiles, 2, half, TILE), f32),
            pltpu.VMEM((tiles, 2, 2, half, TILE), bf),
            pltpu.VMEM((2,) + chunks, f32),
            pltpu.VMEM((2,) + chunks, bf),
            pltpu.VMEM((2,) + chunks, bf),
            pltpu.VMEM((2,) + chunks, bf),
            pltpu.VMEM((2,) + chunks, bf),
            pltpu.VMEM(chunks, bf),
            pltpu.VMEM((steps, half, part), bf),
            pltpu.VMEM((steps, half, part), bf),
            dma((2, 4)), dma, dma((2, 2)), dma((2, 2)), dma((2,)), dma((2, 2)), dma((2, 2)),
            dma((tiles,)), dma((tiles,)), dma((tiles,)), dma((tiles,)),
            dma((2, steps)), dma((2, steps)), dma((2, steps)), dma((2, steps)),
            dma((steps,)), dma((steps,)), dma((steps,)),
        ],
        compiler_params=pltpu.CompilerParams(
            collective_id=0, has_side_effects=True, vmem_limit_bytes=60 * 2**20
        ),
        cost_estimate=pl.CostEstimate(
            flops=2 * flops, bytes_accessed=4 * rows * width, transcendentals=half * width
        ),
    )(tokens, gate_weight, up_weight, gate_mask, up_mask, cotangent)
    step = 512
    grid = rows // step
    mask_spec = pl.BlockSpec(gate_mask.shape, lambda i: (0, 0))
    out_spec = pl.BlockSpec((step, width), lambda i: (i, 0))
    hid_spec = pl.BlockSpec((half // grid, width), lambda i: (i, 0))
    in_spec = pl.BlockSpec((half // grid, kk), lambda i: (i, 0))
    grad_gate, grad_up, hidden, grad_input = pl.pallas_call(
        weight_kernel,
        grid=(grid,),
        out_shape=(
            jax.ShapeDtypeStruct((rows, width), bf),
            jax.ShapeDtypeStruct((rows, width), bf),
            jax.ShapeDtypeStruct((half, width), bf),
            jax.ShapeDtypeStruct((half, kk), bf),
        ),
        in_specs=[
            pl.BlockSpec((step, 2 * half), lambda i: (i, 0)),
            pl.BlockSpec((2, 2 * half, width), lambda i: (0, 0, 0)),
            mask_spec,
            mask_spec,
            hid_spec,
            in_spec,
        ],
        out_specs=(out_spec, out_spec, hid_spec, in_spec),
        scratch_shapes=[pltpu.VMEM((2, rows // BLOCK, width), f32)],
        compiler_params=pltpu.CompilerParams(vmem_limit_bytes=63 * 2**20),
        cost_estimate=pl.CostEstimate(flops=flops, bytes_accessed=4 * rows * width, transcendentals=0),
    )(xt, d.reshape(2, 2 * half, width), gate_mask, up_mask, hidden, grad_input)
    return (hidden, grad_input, grad_gate, grad_up)


def body(mesh):
    return kernel_shards if mesh.shape["tensor"] == 8 and mesh.shape["dp"] == 2 else shards


def solution(mesh):
    in_specs = (
        P(("groups", "dp"), "tensor"),
        P("dp", "tensor"),
        P("dp", "tensor"),
        P("dp", "tensor"),
        P("dp", "tensor"),
        P(("groups", "dp"), "tensor"),
    )
    out_specs = (
        P(("groups", "dp"), "tensor"),
        P(("groups", "dp"), "tensor"),
        P("dp", ("groups", "tensor")),
        P("dp", ("groups", "tensor")),
    )
    return jax.shard_map(body(mesh), mesh=mesh, in_specs=in_specs, out_specs=out_specs, check_vma=False)
```
